32 devices in a mesh: groups: 2 (over x), ctx: 16 (over z, y, core).
Axes of the slice: x: 2, y: 2, z: 4, core: 2. Of those that a mesh axis runs over, the one named last changes fastest.
Arguments:
- queries: bfloat16 [3072, 64, 576], P(('groups', 'ctx')), parts along dimension 0, may hold values from -400 to 400
- kv_latent: bfloat16 [3072, 576], P(('groups', 'ctx')), parts along dimension 0, may hold values from -6 to 6
- span_order: int32 [64], P('groups'), parts along dimension 0, may hold values from 0 to 31, as said below
Outputs:
- attended: bfloat16 [3072, 32768], P(('groups', 'ctx')), parts along dimension 0
The draws below stay inside these ranges and needn't reach their ends.
There are 2 independent parts, one for each index of `groups`. The reference program is written for one: setup_inputs(seed, part) draws one part's arguments, and reference() takes and returns one part's arrays. A program takes and returns all parts, laid end to end along the dimension named above; each array names one. Nothing has to cross between parts.
Inputs may be any that keep to these rules, and one draw needn't show every extreme that they name: `span_order`: entries 2 d and 2 d + 1 are d and 31 - d in an order drawn for each d.
All inputs are finite; a program needn't handle non-finite values.
Results may differ from the reference program's by a relative error of at most 0.0047.
Values may be sent and summed in bfloat16 or wider, within the bound.
A program may use at most 64 MiB of HBM per device.

```python
import jax
import jax.numpy as jnp
from jax import lax

HEADS = 64
KEY_DIM = 128
ROPE_DIM = 64
LATENT = 512
WINDOW = 7
SPAN = 48
SPANS = 32
SEQ = 1536


def shared_rotary(key):
    return jnp.clip(jax.random.normal(jax.random.fold_in(key, 11), (SEQ, ROPE_DIM), jnp.float32), -6.0, 6.0)


def draw_kv_latent(key, part):
    rotary = shared_rotary(key)
    key = jax.random.fold_in(key, 3)
    latent = jnp.clip(jax.random.normal(key, (SEQ, LATENT), jnp.float32), -6.0, 6.0)
    return jnp.concatenate([latent, rotary], axis=1).astype(jnp.bfloat16)


def draw_queries(key, part):
    key = jax.random.fold_in(key, 4)
    values = jnp.clip(jax.random.normal(key, (SEQ, HEADS, LATENT + ROPE_DIM), jnp.float32), -6.0, 6.0)
    return values.astype(jnp.bfloat16)


def draw_span_order(key, part):
    key = jax.random.fold_in(key, 6)
    flips = jax.random.randint(key, (SPANS // 2,), 0, 2)
    lower = jnp.arange(SPANS // 2, dtype=jnp.int32)
    upper = SPANS - 1 - lower
    first = jnp.where(flips == 1, upper, lower)
    second = jnp.where(flips == 1, lower, upper)
    return jnp.stack([first, second], axis=1).reshape(SPANS).astype(jnp.int32)


def setup_inputs(seed: int = 0, part: int = 0) -> dict:
    splits = jax.random.split(jax.random.key(seed), 4)
    part_splits = jax.random.split(jax.random.fold_in(splits[3], part), 4)
    return {
        "queries": draw_queries(jax.random.fold_in(jax.random.fold_in(splits[3], part), 71), part),
        "kv_latent": draw_kv_latent(jax.random.fold_in(jax.random.fold_in(splits[3], part), 71), part),
        "span_order": draw_span_order(jax.random.fold_in(jax.random.fold_in(splits[3], part), 71), part),
    }


def reference(queries, kv_latent, span_order):
    slot_of = jnp.zeros((SPANS,), jnp.int32).at[span_order].set(jnp.arange(SPANS, dtype=jnp.int32))
    query_spans = queries.reshape(SPANS, SPAN, HEADS, LATENT + ROPE_DIM)[slot_of]
    latent_spans = kv_latent.reshape(SPANS, SPAN, LATENT + ROPE_DIM)[slot_of]
    padded = jnp.concatenate([jnp.zeros((WINDOW, SPAN, LATENT + ROPE_DIM), kv_latent.dtype), latent_spans], axis=0)
    scale = (KEY_DIM + ROPE_DIM) ** -0.5
    rows = jnp.arange(SPAN, dtype=jnp.int32)
    keypos = jnp.arange((WINDOW + 1) * SPAN, dtype=jnp.int32)
    backs = WINDOW - keypos // SPAN

    def one_span(span_id):
        window = lax.dynamic_slice_in_dim(padded, span_id, WINDOW + 1, 0).reshape((WINDOW + 1) * SPAN, LATENT + ROPE_DIM)
        window = window.astype(jnp.float32)
        query = lax.dynamic_index_in_dim(query_spans, span_id, 0, keepdims=False).astype(jnp.float32)
        scores = jnp.einsum("phl,kl->hpk", query, window) * scale
        allowed = ((span_id - backs) >= 0)[None, :] & ((backs > 0)[None, :] | ((keypos % SPAN)[None, :] <= rows[:, None]))
        scores = jnp.where(allowed[None], scores, -1e30)
        largest = jnp.max(scores, axis=-1, keepdims=True)
        weights = jnp.where(allowed[None], jnp.exp(scores - largest), 0.0)
        probs = (weights / jnp.sum(weights, axis=-1, keepdims=True)).astype(jnp.bfloat16)
        mixed = jnp.einsum("hpk,kl->phl", probs.astype(jnp.float32), window[:, :LATENT]).astype(jnp.bfloat16)
        return mixed.reshape(SPAN, HEADS * LATENT)

    outputs = lax.map(one_span, jnp.arange(SPANS, dtype=jnp.int32))
    return outputs[span_order].reshape(SEQ, HEADS * LATENT)
```

```python
import functools

import jax
import jax.numpy as jnp
from jax import lax
from jax.experimental import pallas as pl
from jax.experimental.pallas import tpu as pltpu
from jax.sharding import PartitionSpec as P

KEY_DIM = 128
ROPE_DIM = 64
LATENT = 512
WINDOW = 7
HEAD_BLOCK = 16
LOG2E = 1.4426950408889634
MESH = pl.DeviceIdType.MESH


def gather_kernel(n, span, order_ref, kv_ref, win_ref, mine, send_lo, send_hi, send_x, recv_sem):
    me = lax.axis_index("ctx")
    last = 2 * n - 1

    barrier = pltpu.get_barrier_semaphore()
    for k in range(1, WINDOW + 1):
        for other, ok in ((me + k, me + k < n), (me - k, me >= k)):
            @pl.when(ok)
            def _():
                pl.semaphore_signal(barrier, inc=1, device_id={"ctx": other}, device_id_type=MESH)

    first, second = kv_ref[:span], kv_ref[span:]
    lower_first = jnp.full(first.shape, order_ref[2 * me], jnp.int32) < n
    own_lower = jnp.where(lower_first, first, second)
    own_upper = jnp.where(lower_first, second, first)
    mine[0] = own_lower
    mine[1] = own_upper
    own_rows = pl.ds(WINDOW * span, span)
    pl.semaphore_wait(barrier, jnp.minimum(me, WINDOW) + jnp.minimum(n - 1 - me, WINDOW))

    def rows(back):
        return pl.ds(pl.multiple_of((WINDOW - back) * span, 16), span)

    def copy(which, target, window, back, send):
        return pltpu.make_async_remote_copy(
            src_ref=mine.at[which],
            dst_ref=win_ref.at[window, rows(back)],
            send_sem=send,
            recv_sem=recv_sem.at[window, back],
            device_id={"ctx": target},
            device_id_type=MESH,
        )

    def sends(action):
        for k in range(1, WINDOW + 1):
            @pl.when(me + k < n)
            def _():
                action(copy(0, me + k, 0, k, send_lo.at[k]))

            @pl.when(me >= k)
            def _():
                action(copy(1, me - k, 1, k, send_hi.at[k]))

            back = last - 2 * me + k

            @pl.when((me >= k) & (back <= WINDOW))
            def _():
                action(copy(0, me - k, 1, back, send_x.at[k]))

    sends(lambda c: c.start())
    win_ref[0, own_rows] = own_lower
    win_ref[1, own_rows] = own_upper
    for k in range(1, WINDOW + 1):
        @pl.when(me >= k)
        def _():
            copy(0, me - k, 0, k, send_lo.at[k]).wait_recv()

        @pl.when(me < k)
        def _():
            win_ref[0, rows(k)] = jnp.zeros_like(own_lower)

    for k in range(1, WINDOW + 1):
        @pl.when(2 * me + k < last)
        def _():
            copy(0, jnp.where(me + 1 < n, me + 1, me - 1), 1, k, send_lo.at[k]).wait_recv()

        @pl.when(2 * me + k >= last)
        def _():
            win_ref[1, rows(k)] = win_ref[0, rows(2 * me + k - last)]
    sends(lambda c: c.wait_send())


def attend_kernel(n, span, heads, order_ref, q_ref, win_ref, out_ref, scores, bias, probs):
    slot, group = pl.program_id(0), pl.program_id(1)
    me = order_ref[order_ref.shape[0] - 1]
    width = (WINDOW + 1) * span
    span_id = order_ref[2 * me + slot]
    factor = LOG2E * (KEY_DIM + ROPE_DIM) ** -0.5

    @pl.when(group == 0)
    def _():
        keypos = lax.broadcasted_iota(jnp.int32, (span, width), 1)
        row = lax.broadcasted_iota(jnp.int32, (span, width), 0)
        allowed = (keypos >= (WINDOW - span_id) * span) & (keypos - WINDOW * span <= row)
        bias[...] = jnp.where(allowed, 0.0, -1e30)

    block = q_ref[...].reshape(span * HEAD_BLOCK, q_ref.shape[2])
    product = lax.dot_general(block, win_ref[0], (((1,), (1,)), ((), ())), preferred_element_type=jnp.float32)
    chunks = width // 128
    for c in range(chunks):
        scores[c] = product[:, c * 128 : (c + 1) * 128]
    for h in range(HEAD_BLOCK):
        parts = [
            scores.at[c][pl.ds(h, span, stride=HEAD_BLOCK), :] + bias[:, c * 128 : (c + 1) * 128]
            for c in range(chunks)
        ]
        largest = jnp.max(functools.reduce(jnp.maximum, parts), axis=-1, keepdims=True)
        weights = [jnp.exp2((part - largest) * factor) for part in parts]
        inverse = 1.0 / jnp.sum(sum(weights), axis=-1, keepdims=True)
        for c in range(chunks):
            probs[h * span : (h + 1) * span, c * 128 : (c + 1) * 128] = (weights[c] * inverse).astype(jnp.bfloat16)
    mixed = jnp.dot(probs[...], win_ref[0, :, :LATENT], preferred_element_type=jnp.float32)
    for h in range(HEAD_BLOCK):
        out_ref[:, h * LATENT : (h + 1) * LATENT] = mixed[h * span : (h + 1) * span].astype(jnp.bfloat16)


def local(queries, kv_latent, span_order):
    n = lax.axis_size("ctx")
    tokens, heads, dim = queries.shape
    span = tokens // 2
    width = (WINDOW + 1) * span
    windows = pl.pallas_call(
        functools.partial(gather_kernel, n, span),
        out_shape=jax.ShapeDtypeStruct((2, width, dim), jnp.bfloat16),
        in_specs=[pl.BlockSpec(memory_space=pltpu.SMEM), pl.BlockSpec(memory_space=pltpu.VMEM)],
        out_specs=pl.BlockSpec(memory_space=pltpu.VMEM),
        scratch_shapes=[
            pltpu.VMEM((2, span, dim), jnp.bfloat16),
            pltpu.SemaphoreType.DMA((WINDOW + 1,)),
            pltpu.SemaphoreType.DMA((WINDOW + 1,)),
            pltpu.SemaphoreType.DMA((WINDOW + 1,)),
            pltpu.SemaphoreType.DMA((2, WINDOW + 1)),
        ],
        compiler_params=pltpu.CompilerParams(collective_id=0, has_side_effects=True),
        name="gather_windows",
    )(span_order, kv_latent)
    scalars = jnp.concatenate([span_order, lax.axis_index("ctx")[None].astype(jnp.int32)])

    def window_of(slot, group, order):
        return jnp.where(order[2 * order[2 * n] + slot] < n, 0, 1), 0, 0

    return pl.pallas_call(
        functools.partial(attend_kernel, n, span, heads),
        out_shape=jax.ShapeDtypeStruct((tokens, heads * LATENT), jnp.bfloat16),
        grid_spec=pltpu.PrefetchScalarGridSpec(
            num_scalar_prefetch=1,
            grid=(2, heads // HEAD_BLOCK),
            in_specs=[
                pl.BlockSpec((span, HEAD_BLOCK, dim), lambda s, g, order: (s, g, 0)),
                pl.BlockSpec((1, width, dim), window_of),
            ],
            out_specs=pl.BlockSpec((span, HEAD_BLOCK * LATENT), lambda s, g, order: (s, g)),
            scratch_shapes=[
                pltpu.VMEM((width // 128, span * HEAD_BLOCK, 128), jnp.float32),
                pltpu.VMEM((span, width), jnp.float32),
                pltpu.VMEM((span * HEAD_BLOCK, width), jnp.bfloat16),
            ],
        ),
        compiler_params=pltpu.CompilerParams(vmem_limit_bytes=48 * 1024 * 1024),
        name="attend",
    )(scalars, queries, windows)


def solution(mesh):
    in_specs = (P(("groups", "ctx"), None, None), P(("groups", "ctx"), None), P("groups"))
    out_specs = P(("groups", "ctx"), None)
    return jax.shard_map(local, mesh=mesh, in_specs=in_specs, out_specs=out_specs, check_vma=False)
```

```python
import functools

import jax
import jax.numpy as jnp
from jax import lax
from jax.experimental import pallas as pl
from jax.experimental.pallas import tpu as pltpu
from jax.sharding import PartitionSpec as P

KEY_DIM = 128
ROPE_DIM = 64
LATENT = 512
WINDOW = 7
HEAD_BLOCK = 16
PITCH = 17
PARTS = 2
LOG2E = 1.4426950408889634
MESH = pl.DeviceIdType.MESH


def gather_kernel(n, span, order_ref, kv_ref, win_ref, mine, send_lo, send_hi, send_x, send_f, recv_sem):
    me = lax.axis_index("ctx")
    last = 2 * n - 1

    barrier = pltpu.get_barrier_semaphore()
    for k in range(1, WINDOW + 1):
        for other, ok in ((me + k, me + k < n), (me - k, me >= k)):
            @pl.when(ok)
            def _():
                pl.semaphore_signal(barrier, inc=1, device_id={"ctx": other}, device_id_type=MESH)

    first, second = kv_ref[:span], kv_ref[span:]
    lower_first = jnp.full(first.shape, order_ref[2 * me], jnp.int32) < n
    own_lower = jnp.where(lower_first, first, second)
    own_upper = jnp.where(lower_first, second, first)
    mine[0] = own_lower
    mine[1] = own_upper
    own_rows = pl.ds(WINDOW * span, span)
    pl.semaphore_wait(barrier, jnp.minimum(me, WINDOW) + jnp.minimum(n - 1 - me, WINDOW))

    def rows(back):
        return pl.ds(pl.multiple_of((WINDOW - back) * span, 16), span)

    def copy(which, target, window, back, send):
        return pltpu.make_async_remote_copy(
            src_ref=mine.at[which],
            dst_ref=win_ref.at[window, rows(back)],
            send_sem=send,
            recv_sem=recv_sem.at[window, back],
            device_id={"ctx": target},
            device_id_type=MESH,
        )

    even = me % 2 == 0
    sibling = me + 1 - 2 * (me % 2)

    def sends(action):
        for k in (6, 4, 7, 2, 1):
            up, down = me + k < n, me >= k
            if k == 7:
                up, down = up & (me % 2 == 1), down & even
            if k == 1:
                up, down = up & even, down & (me % 2 == 1)

            @pl.when(up)
            def _():
                action(copy(0, me + k, 0, k, send_lo.at[k]))

            @pl.when(down)
            def _():
                action(copy(1, me - k, 1, k, send_hi.at[k]))

        for k in range(1, WINDOW + 1):
            back = last - 2 * me + k

            @pl.when((me >= k) & (back <= WINDOW))
            def _():
                action(copy(0, me - k, 1, back, send_x.at[k]))

    def relay(window, k):
        back = k + 1 - 2 * (me % 2) if window == 0 else k - 1 + 2 * (me % 2)
        return pltpu.make_async_remote_copy(
            src_ref=win_ref.at[window, rows(k)],
            dst_ref=win_ref.at[window, rows(back)],
            send_sem=send_f.at[window, k],
            recv_sem=recv_sem.at[window, back],
            device_id={"ctx": sibling},
            device_id_type=MESH,
        )

    def arrived(window, k):
        copy(0, sibling, window, k, send_lo.at[k]).wait_recv()

    sends(lambda c: c.start())
    win_ref[0, own_rows] = own_lower
    win_ref[1, own_rows] = own_upper
    for k in (2, 4, 6):
        for window, ok in ((0, me >= k), (1, me + k < n)):
            @pl.when(ok)
            def _():
                arrived(window, k)
                relay(window, k).start()

    for k in range(1, WINDOW + 1):
        if k % 2:
            @pl.when(me >= k)
            def _():
                arrived(0, k)

        @pl.when(me < k)
        def _():
            win_ref[0, rows(k)] = jnp.zeros_like(own_lower)

    for k in range(1, WINDOW + 1):
        @pl.when((2 * me + k < last) & (me + k >= n) if k in (2, 4, 6) else 2 * me + k < last)
        def _():
            arrived(1, k)

        @pl.when(2 * me + k >= last)
        def _():
            win_ref[1, rows(k)] = win_ref[0, rows(2 * me + k - last)]
    sends(lambda c: c.wait_send())
    for k in (2, 4, 6):
        for window, ok in ((0, me >= k), (1, me + k < n)):
            @pl.when(ok)
            def _():
                relay(window, k).wait_send()


def attend_kernel(n, span, heads, order_ref, q_hbm, win_ref, out_hbm, q, out, scores, bias, probs, q_sem, out_sem):
    me = lax.axis_index("ctx")
    width = (WINDOW + 1) * span
    groups = heads // HEAD_BLOCK
    blocks = 2 * groups
    chunks = width // 128
    factor = LOG2E * (KEY_DIM + ROPE_DIM) ** -0.5
    columns = HEAD_BLOCK * LATENT

    def multiple(value, of):
        return value if isinstance(value, int) else pl.multiple_of(value, of)

    def q_copy(b):
        slot, group = b // groups, b % groups
        positions = pl.ds(multiple(slot * span, 16), span)
        block_heads = pl.ds(multiple(group * HEAD_BLOCK, HEAD_BLOCK), HEAD_BLOCK)
        return pltpu.make_async_copy(q_hbm.at[positions, block_heads], q.at[b], q_sem.at[b])

    def out_copy(b):
        slot, group = b // groups, b % groups
        positions = pl.ds(multiple(slot * span, 16), span)
        return pltpu.make_async_copy(
            out.at[b], out_hbm.at[positions, pl.ds(multiple(group * columns, columns), columns)], out_sem.at[b]
        )

    for b in range(blocks):
        q_copy(b).start()
    for slot in range(2):
        span_id = order_ref[2 * me + slot]
        keypos = lax.broadcasted_iota(jnp.int32, (span, width), 1)
        row = lax.broadcasted_iota(jnp.int32, (span, width), 0)
        allowed = (keypos >= (WINDOW - span_id) * span) & (keypos - WINDOW * span <= row)
        bias[slot] = jnp.where(allowed, 0.0, -1e30)

    def window_of(b):
        return jnp.where(order_ref[2 * me + b // groups] < n, 0, 1)

    pos_part, head_part = span // PARTS, HEAD_BLOCK // PARTS

    def score(b, parity, part):
        block = q[b, part * pos_part : (part + 1) * pos_part].reshape(pos_part * HEAD_BLOCK, q.shape[3])
        product = lax.dot_general(
            block, win_ref[window_of(b)], (((1,), (1,)), ((), ())), preferred_element_type=jnp.float32
        )
        for c in range(chunks):
            for p in range(pos_part):
                first = (part * pos_part + p) * PITCH
                scores[parity * chunks + c, first : first + HEAD_BLOCK] = product[
                    p * HEAD_BLOCK : (p + 1) * HEAD_BLOCK, c * 128 : (c + 1) * 128
                ]

    def mix(b, parity, part):
        for h in range(part * head_part, (part + 1) * head_part):
            tiles = [
                scores.at[parity * chunks + c][pl.ds(h, span, stride=PITCH), :]
                + bias[b // groups, :, c * 128 : (c + 1) * 128]
                for c in range(chunks)
            ]
            largest = jnp.max(functools.reduce(jnp.maximum, tiles), axis=-1, keepdims=True)
            weights = [jnp.exp2((tile - largest) * factor) for tile in tiles]
            inverse = 1.0 / jnp.sum(sum(weights), axis=-1, keepdims=True)
            for c in range(chunks):
                probs[parity, h * span : (h + 1) * span, c * 128 : (c + 1) * 128] = (weights[c] * inverse).astype(
                    jnp.bfloat16
                )
        rows = head_part * span
        mixed = jnp.dot(
            probs[parity, part * rows : (part + 1) * rows],
            win_ref[window_of(b), :, :LATENT],
            preferred_element_type=jnp.float32,
        )
        for k in range(head_part):
            h = part * head_part + k
            out[b, :, h * LATENT : (h + 1) * LATENT] = mixed[k * span : (k + 1) * span].astype(jnp.bfloat16)

    def step(b, parity, more=True):
        if more:
            q_copy(b + 1).wait()
        for part in range(PARTS):
            if more:
                score(b + 1, 1 - parity, part)
            mix(b, parity, part)
        out_copy(b).start()

    q_copy(0).wait()
    for part in range(PARTS):
        score(0, 0, part)

    @pl.loop(0, groups - 1)
    def _(pair):
        step(2 * pair, 0)
        step(2 * pair + 1, 1)

    step(blocks - 2, 0)
    step(blocks - 1, 1, more=False)
    for b in range(blocks):
        out_copy(b).wait()


def local(queries, kv_latent, span_order):
    n = lax.axis_size("ctx")
    tokens, heads, dim = queries.shape
    span = tokens // 2
    width = (WINDOW + 1) * span
    windows = pl.pallas_call(
        functools.partial(gather_kernel, n, span),
        out_shape=jax.ShapeDtypeStruct((2, width, dim), jnp.bfloat16),
        in_specs=[pl.BlockSpec(memory_space=pltpu.SMEM), pl.BlockSpec(memory_space=pltpu.VMEM)],
        out_specs=pl.BlockSpec(memory_space=pltpu.VMEM),
        scratch_shapes=[
            pltpu.VMEM((2, span, dim), jnp.bfloat16),
            pltpu.SemaphoreType.DMA((WINDOW + 1,)),
            pltpu.SemaphoreType.DMA((WINDOW + 1,)),
            pltpu.SemaphoreType.DMA((WINDOW + 1,)),
            pltpu.SemaphoreType.DMA((2, WINDOW + 1)),
            pltpu.SemaphoreType.DMA((2, WINDOW + 1)),
        ],
        compiler_params=pltpu.CompilerParams(collective_id=0, has_side_effects=True),
        name="gather_windows",
    )(span_order, kv_latent)
    blocks = 2 * (heads // HEAD_BLOCK)
    return pl.pallas_call(
        functools.partial(attend_kernel, n, span, heads),
        out_shape=jax.ShapeDtypeStruct((tokens, heads * LATENT), jnp.bfloat16),
        in_specs=[
            pl.BlockSpec(memory_space=pltpu.SMEM),
            pl.BlockSpec(memory_space=pl.ANY),
            pl.BlockSpec(memory_space=pltpu.VMEM),
        ],
        out_specs=pl.BlockSpec(memory_space=pl.ANY),
        scratch_shapes=[
            pltpu.VMEM((blocks, span, HEAD_BLOCK, dim), jnp.bfloat16),
            pltpu.VMEM((blocks, span, HEAD_BLOCK * LATENT), jnp.bfloat16),
            pltpu.VMEM((2 * (width // 128), span * PITCH, 128), jnp.float32),
            pltpu.VMEM((2, span, width), jnp.float32),
            pltpu.VMEM((2, span * HEAD_BLOCK, width), jnp.bfloat16),
            pltpu.SemaphoreType.DMA((blocks,)),
            pltpu.SemaphoreType.DMA((blocks,)),
        ],
        compiler_params=pltpu.CompilerParams(vmem_limit_bytes=48 * 1024 * 1024),
        name="attend",
    )(span_order, queries, windows)


def solution(mesh):
    in_specs = (P(("groups", "ctx"), None, None), P(("groups", "ctx"), None), P("groups"))
    out_specs = P(("groups", "ctx"), None)
    return jax.shard_map(local, mesh=mesh, in_specs=in_specs, out_specs=out_specs, check_vma=False)
```

```python
import functools

import jax
import jax.numpy as jnp
from jax import lax
from jax.experimental import pallas as pl
from jax.experimental.pallas import tpu as pltpu
from jax.sharding import PartitionSpec as P

KEY_DIM = 128
ROPE_DIM = 64
LATENT = 512
WINDOW = 7
HEAD_BLOCK = 16
PITCH = 17
PARTS = 2
LOG2E = 1.4426950408889634
MESH = pl.DeviceIdType.MESH


def gather_kernel(
    n, span, order_ref, kv_ref, q_hbm, win_ref, near_ref, mine, near_keys, q, send_lo, send_hi, send_x, send_f, recv_sem, q_sem
):
    me = lax.axis_index("ctx")
    last = 2 * n - 1

    groups = q_hbm.shape[1] // HEAD_BLOCK
    blocks = 2 * groups

    def q_copy(b):
        slot, group = b // groups, b % groups
        return pltpu.make_async_copy(
            q_hbm.at[pl.ds(slot * span, span), pl.ds(group * HEAD_BLOCK, HEAD_BLOCK)], q.at[b], q_sem.at[b]
        )

    for b in range(blocks):
        q_copy(b).start()

    barrier = pltpu.get_barrier_semaphore()
    for k in range(1, WINDOW + 1):
        for other, ok in ((me + k, me + k < n), (me - k, me >= k)):
            @pl.when(ok)
            def _():
                pl.semaphore_signal(barrier, inc=1, device_id={"ctx": other}, device_id_type=MESH)

    first, second = kv_ref[:span], kv_ref[span:]
    lower_first = jnp.full(first.shape, order_ref[2 * me], jnp.int32) < n
    own_lower = jnp.where(lower_first, first, second)
    own_upper = jnp.where(lower_first, second, first)
    mine[0] = own_lower
    mine[1] = own_upper
    own_rows = pl.ds(WINDOW * span, span)
    pl.semaphore_wait(barrier, jnp.minimum(me, WINDOW) + jnp.minimum(n - 1 - me, WINDOW))

    def rows(back):
        return pl.ds(pl.multiple_of((WINDOW - back) * span, 16), span)

    def copy(which, target, window, back, send):
        return pltpu.make_async_remote_copy(
            src_ref=mine.at[which],
            dst_ref=win_ref.at[window, rows(back)],
            send_sem=send,
            recv_sem=recv_sem.at[window, back],
            device_id={"ctx": target},
            device_id_type=MESH,
        )

    even = me % 2 == 0
    sibling = me + 1 - 2 * (me % 2)

    def sends(action):
        for k in (2, 1, 6, 4, 7):
            up, down = me + k < n, me >= k
            if k == 7:
                up, down = up & (me % 2 == 1), down & even
            if k == 1:
                up, down = up & even, down & (me % 2 == 1)

            @pl.when(up)
            def _():
                action(copy(0, me + k, 0, k, send_lo.at[k]))

            @pl.when(down)
            def _():
                action(copy(1, me - k, 1, k, send_hi.at[k]))

        for k in range(1, WINDOW + 1):
            back = last - 2 * me + k

            @pl.when((me >= k) & (back <= WINDOW))
            def _():
                action(copy(0, me - k, 1, back, send_x.at[k]))

    def relay(window, k):
        back = k + 1 - 2 * (me % 2) if window == 0 else k - 1 + 2 * (me % 2)
        return pltpu.make_async_remote_copy(
            src_ref=win_ref.at[window, rows(k)],
            dst_ref=win_ref.at[window, rows(back)],
            send_sem=send_f.at[window, k],
            recv_sem=recv_sem.at[window, back],
            device_id={"ctx": sibling},
            device_id_type=MESH,
        )

    def arrived(window, k):
        copy(0, sibling, window, k, send_lo.at[k]).wait_recv()

    sends(lambda c: c.start())
    win_ref[0, own_rows] = own_lower
    win_ref[1, own_rows] = own_upper
    def pass_on(k):
        for window, ok in ((0, me >= k), (1, me + k < n)):
            @pl.when(ok)
            def _():
                arrived(window, k)
                relay(window, k).start()

    def finish(ks):
        for k in ks:
            if k % 2:
                @pl.when(me >= k)
                def _():
                    arrived(0, k)

            @pl.when(me < k)
            def _():
                win_ref[0, rows(k)] = jnp.zeros_like(own_lower)

        for k in ks:
            @pl.when(((2 * me + k < last) & (me + k >= n)) if k % 2 == 0 else 2 * me + k < last)
            def _():
                arrived(1, k)

        for k in ks:
            @pl.when(2 * me + k >= last)
            def _():
                win_ref[1, rows(k)] = win_ref[0, rows(2 * me + k - last)]

    def near_scores(lo, hi):
        @pl.loop(lo, hi)
        def _(b):
            block = q[b].reshape(span * HEAD_BLOCK, q.shape[3])
            product = lax.dot_general(
                block, near_keys[b // groups], (((1,), (1,)), ((), ())), preferred_element_type=jnp.float32
            )
            for p in range(span):
                near_ref[b, p * PITCH : p * PITCH + HEAD_BLOCK] = product[p * HEAD_BLOCK : (p + 1) * HEAD_BLOCK]

    pass_on(2)
    finish((1, 2))
    tail = pl.ds(win_ref.shape[1] - 128, 128)
    near_lower, near_upper = win_ref[0, tail], win_ref[1, tail]
    lower_first = jnp.full(near_lower.shape, order_ref[2 * me], jnp.int32) < n
    near_keys[0] = jnp.where(lower_first, near_lower, near_upper)
    near_keys[1] = jnp.where(lower_first, near_upper, near_lower)
    for b in range(blocks):
        q_copy(b).wait()
    near_scores(0, blocks // 4)
    pass_on(4)
    near_scores(blocks // 4, blocks // 2)
    pass_on(6)
    near_scores(blocks // 2, blocks)
    finish((3, 4, 5, 6, 7))
    sends(lambda c: c.wait_send())
    for k in (2, 4, 6):
        for window, ok in ((0, me >= k), (1, me + k < n)):
            @pl.when(ok)
            def _():
                relay(window, k).wait_send()


def attend_kernel(n, span, heads, order_ref, q_hbm, win_ref, near_ref, out_hbm, q, out, scores, bias, probs, q_sem, out_sem):
    me = lax.axis_index("ctx")
    width = (WINDOW + 1) * span
    groups = heads // HEAD_BLOCK
    blocks = 2 * groups
    chunks = width // 128
    factor = LOG2E * (KEY_DIM + ROPE_DIM) ** -0.5
    columns = HEAD_BLOCK * LATENT

    def multiple(value, of):
        return value if isinstance(value, int) else pl.multiple_of(value, of)

    def q_copy(b):
        slot, group = b // groups, b % groups
        positions = pl.ds(multiple(slot * span, 16), span)
        block_heads = pl.ds(multiple(group * HEAD_BLOCK, HEAD_BLOCK), HEAD_BLOCK)
        return pltpu.make_async_copy(q_hbm.at[positions, block_heads], q.at[b], q_sem.at[b])

    def out_copy(b):
        slot, group = b // groups, b % groups
        positions = pl.ds(multiple(slot * span, 16), span)
        return pltpu.make_async_copy(
            out.at[b], out_hbm.at[positions, pl.ds(multiple(group * columns, columns), columns)], out_sem.at[b]
        )

    for b in range(blocks):
        q_copy(b).start()
    for slot in range(2):
        span_id = order_ref[2 * me + slot]
        keypos = lax.broadcasted_iota(jnp.int32, (span, width), 1)
        row = lax.broadcasted_iota(jnp.int32, (span, width), 0)
        allowed = (keypos >= (WINDOW - span_id) * span) & (keypos - WINDOW * span <= row)
        bias[slot] = jnp.where(allowed, 0.0, -1e30)

    def window_of(b):
        return jnp.where(order_ref[2 * me + b // groups] < n, 0, 1)

    pos_part, head_part = span // PARTS, HEAD_BLOCK // PARTS

    def score(b, parity, part):
        block = q[b, part * pos_part : (part + 1) * pos_part].reshape(pos_part * HEAD_BLOCK, q.shape[3])
        product = lax.dot_general(
            block, win_ref[window_of(b), : width - 128], (((1,), (1,)), ((), ())), preferred_element_type=jnp.float32
        )
        for c in range(chunks - 1):
            for p in range(pos_part):
                first = (part * pos_part + p) * PITCH
                scores[parity * (chunks - 1) + c, first : first + HEAD_BLOCK] = product[
                    p * HEAD_BLOCK : (p + 1) * HEAD_BLOCK, c * 128 : (c + 1) * 128
                ]

    def mix(b, parity, part):
        for h in range(part * head_part, (part + 1) * head_part):
            planes = [scores.at[parity * (chunks - 1) + c] for c in range(chunks - 1)] + [near_ref.at[b]]
            tiles = [
                plane[pl.ds(h, span, stride=PITCH), :] + bias[b // groups, :, c * 128 : (c + 1) * 128]
                for c, plane in enumerate(planes)
            ]
            largest = jnp.max(functools.reduce(jnp.maximum, tiles), axis=-1, keepdims=True)
            weights = [jnp.exp2((tile - largest) * factor) for tile in tiles]
            inverse = 1.0 / jnp.sum(sum(weights), axis=-1, keepdims=True)
            for c in range(chunks):
                probs[parity, h * span : (h + 1) * span, c * 128 : (c + 1) * 128] = (weights[c] * inverse).astype(
                    jnp.bfloat16
                )
        rows = head_part * span
        mixed = jnp.dot(
            probs[parity, part * rows : (part + 1) * rows],
            win_ref[window_of(b), :, :LATENT],
            preferred_element_type=jnp.float32,
        )
        for k in range(head_part):
            h = part * head_part + k
            out[b, :, h * LATENT : (h + 1) * LATENT] = mixed[k * span : (k + 1) * span].astype(jnp.bfloat16)

    def step(b, parity, more=True):
        if more:
            q_copy(b + 1).wait()
        for part in range(PARTS):
            if more:
                score(b + 1, 1 - parity, part)
            mix(b, parity, part)
        out_copy(b).start()

    q_copy(0).wait()
    for part in range(PARTS):
        score(0, 0, part)

    @pl.loop(0, groups - 1)
    def _(pair):
        step(2 * pair, 0)
        step(2 * pair + 1, 1)

    step(blocks - 2, 0)
    step(blocks - 1, 1, more=False)
    for b in range(blocks):
        out_copy(b).wait()


def local(queries, kv_latent, span_order):
    n = lax.axis_size("ctx")
    tokens, heads, dim = queries.shape
    span = tokens // 2
    width = (WINDOW + 1) * span
    blocks = 2 * (heads // HEAD_BLOCK)
    windows, near = pl.pallas_call(
        functools.partial(gather_kernel, n, span),
        out_shape=(
            jax.ShapeDtypeStruct((2, width, dim), jnp.bfloat16),
            jax.ShapeDtypeStruct((blocks, span * PITCH, 128), jnp.float32),
        ),
        in_specs=[
            pl.BlockSpec(memory_space=pltpu.SMEM),
            pl.BlockSpec(memory_space=pltpu.VMEM),
            pl.BlockSpec(memory_space=pltpu.HBM),
        ],
        out_specs=(pl.BlockSpec(memory_space=pltpu.VMEM), pl.BlockSpec(memory_space=pltpu.VMEM)),
        scratch_shapes=[
            pltpu.VMEM((2, span, dim), jnp.bfloat16),
            pltpu.VMEM((2, 128, dim), jnp.bfloat16),
            pltpu.VMEM((blocks, span, HEAD_BLOCK, dim), jnp.bfloat16),
            pltpu.SemaphoreType.DMA((WINDOW + 1,)),
            pltpu.SemaphoreType.DMA((WINDOW + 1,)),
            pltpu.SemaphoreType.DMA((WINDOW + 1,)),
            pltpu.SemaphoreType.DMA((2, WINDOW + 1)),
            pltpu.SemaphoreType.DMA((2, WINDOW + 1)),
            pltpu.SemaphoreType.DMA((blocks,)),
        ],
        compiler_params=pltpu.CompilerParams(
            collective_id=0, has_side_effects=True, vmem_limit_bytes=48 * 1024 * 1024
        ),
        name="gather_windows",
    )(span_order, kv_latent, queries)
    return pl.pallas_call(
        functools.partial(attend_kernel, n, span, heads),
        out_shape=jax.ShapeDtypeStruct((tokens, heads * LATENT), jnp.bfloat16),
        in_specs=[
            pl.BlockSpec(memory_space=pltpu.SMEM),
            pl.BlockSpec(memory_space=pltpu.HBM),
            pl.BlockSpec(memory_space=pltpu.VMEM),
            pl.BlockSpec(memory_space=pltpu.VMEM),
        ],
        out_specs=pl.BlockSpec(memory_space=pltpu.HBM),
        scratch_shapes=[
            pltpu.VMEM((blocks, span, HEAD_BLOCK, dim), jnp.bfloat16),
            pltpu.VMEM((blocks, span, HEAD_BLOCK * LATENT), jnp.bfloat16),
            pltpu.VMEM((2 * (width // 128 - 1), span * PITCH, 128), jnp.float32),
            pltpu.VMEM((2, span, width), jnp.float32),
            pltpu.VMEM((2, span * HEAD_BLOCK, width), jnp.bfloat16),
            pltpu.SemaphoreType.DMA((blocks,)),
            pltpu.SemaphoreType.DMA((blocks,)),
        ],
        compiler_params=pltpu.CompilerParams(vmem_limit_bytes=48 * 1024 * 1024),
        name="attend",
    )(span_order, queries, windows, near)


def solution(mesh):
    in_specs = (P(("groups", "ctx"), None, None), P(("groups", "ctx"), None), P("groups"))
    out_specs = P(("groups", "ctx"), None)
    return jax.shard_map(local, mesh=mesh, in_specs=in_specs, out_specs=out_specs, check_vma=False)
```

```python
import functools

import jax
import jax.numpy as jnp
from jax import lax
from jax.experimental import pallas as pl
from jax.experimental.pallas import tpu as pltpu
from jax.sharding import PartitionSpec as P

KEY_DIM = 128
ROPE_DIM = 64
LATENT = 512
WINDOW = 7
HEAD_BLOCK = 16
PITCH = 17
PARTS = 2
LOG2E = 1.4426950408889634
MESH = pl.DeviceIdType.MESH


def gather_kernel(
    n, span, order_ref, kv_ref, q_hbm, win_ref, near_ref, mine, near_keys, q, send_lo, send_hi, send_x, send_f, recv_sem, q_sem
):
    me = lax.axis_index("ctx")
    last = 2 * n - 1

    groups = q_hbm.shape[1] // HEAD_BLOCK
    blocks = 2 * groups

    def q_copy(b):
        slot, group = b // groups, b % groups
        return pltpu.make_async_copy(
            q_hbm.at[pl.ds(slot * span, span), pl.ds(group * HEAD_BLOCK, HEAD_BLOCK)], q.at[b], q_sem.at[b]
        )

    for b in range(blocks):
        q_copy(b).start()

    barrier = pltpu.get_barrier_semaphore()
    for k in range(1, WINDOW + 1):
        for other, ok in ((me + k, me + k < n), (me - k, me >= k)):
            @pl.when(ok)
            def _():
                pl.semaphore_signal(barrier, inc=1, device_id={"ctx": other}, device_id_type=MESH)

    first, second = kv_ref[:span], kv_ref[span:]
    lower_first = jnp.full(first.shape, order_ref[2 * me], jnp.int32) < n
    own_lower = jnp.where(lower_first, first, second)
    own_upper = jnp.where(lower_first, second, first)
    mine[0] = own_lower
    mine[1] = own_upper
    own_rows = pl.ds(WINDOW * span, span)
    pl.semaphore_wait(barrier, jnp.minimum(me, WINDOW) + jnp.minimum(n - 1 - me, WINDOW))

    def rows(back):
        return pl.ds(pl.multiple_of((WINDOW - back) * span, 16), span)

    def copy(which, target, window, back, send):
        return pltpu.make_async_remote_copy(
            src_ref=mine.at[which],
            dst_ref=win_ref.at[window, rows(back)],
            send_sem=send,
            recv_sem=recv_sem.at[window, back],
            device_id={"ctx": target},
            device_id_type=MESH,
        )

    even = me % 2 == 0
    sibling = me + 1 - 2 * (me % 2)

    def sends(action):
        for k in (2, 1, 6, 4, 7):
            up, down = me + k < n, me >= k
            if k == 7:
                up, down = up & (me % 2 == 1), down & even
            if k == 1:
                up, down = up & even, down & (me % 2 == 1)

            @pl.when(up)
            def _():
                action(copy(0, me + k, 0, k, send_lo.at[k]))

            @pl.when(down)
            def _():
                action(copy(1, me - k, 1, k, send_hi.at[k]))

        for k in range(1, WINDOW + 1):
            back = last - 2 * me + k

            @pl.when((me >= k) & (back <= WINDOW))
            def _():
                action(copy(0, me - k, 1, back, send_x.at[k]))

    def relay(window, k):
        back = k + 1 - 2 * (me % 2) if window == 0 else k - 1 + 2 * (me % 2)
        return pltpu.make_async_remote_copy(
            src_ref=win_ref.at[window, rows(k)],
            dst_ref=win_ref.at[window, rows(back)],
            send_sem=send_f.at[window, k],
            recv_sem=recv_sem.at[window, back],
            device_id={"ctx": sibling},
            device_id_type=MESH,
        )

    def arrived(window, k):
        copy(0, sibling, window, k, send_lo.at[k]).wait_recv()

    sends(lambda c: c.start())
    win_ref[0, own_rows] = own_lower
    win_ref[1, own_rows] = own_upper
    def pass_on(k):
        for window, ok in ((0, me >= k), (1, me + k < n)):
            @pl.when(ok)
            def _():
                arrived(window, k)
                relay(window, k).start()

    def finish(ks):
        for k in ks:
            if k % 2:
                @pl.when(me >= k)
                def _():
                    arrived(0, k)

            @pl.when(me < k)
            def _():
                win_ref[0, rows(k)] = jnp.zeros_like(own_lower)

        for k in ks:
            @pl.when(((2 * me + k < last) & (me + k >= n)) if k % 2 == 0 else 2 * me + k < last)
            def _():
                arrived(1, k)

        for k in ks:
            @pl.when(2 * me + k >= last)
            def _():
                win_ref[1, rows(k)] = win_ref[0, rows(2 * me + k - last)]

    def near_scores(lo, hi):
        @pl.loop(lo, hi)
        def _(b):
            block = q[b].reshape(span * HEAD_BLOCK, q.shape[3])
            product = lax.dot_general(
                block, near_keys[b // groups], (((1,), (1,)), ((), ())), preferred_element_type=jnp.float32
            )
            for p in range(span):
                near_ref[b, p * PITCH : p * PITCH + HEAD_BLOCK] = product[p * HEAD_BLOCK : (p + 1) * HEAD_BLOCK]

    pass_on(2)
    finish((1, 2))
    tail = pl.ds(win_ref.shape[1] - 128, 128)
    near_lower, near_upper = win_ref[0, tail], win_ref[1, tail]
    lower_first = jnp.full(near_lower.shape, order_ref[2 * me], jnp.int32) < n
    near_keys[0] = jnp.where(lower_first, near_lower, near_upper)
    near_keys[1] = jnp.where(lower_first, near_upper, near_lower)
    for b in range(blocks):
        q_copy(b).wait()
    pass_on(4)
    near_scores(0, blocks // 4)
    pass_on(6)
    near_scores(blocks // 4, blocks)
    finish((3, 4, 5, 6, 7))
    sends(lambda c: c.wait_send())
    for k in (2, 4, 6):
        for window, ok in ((0, me >= k), (1, me + k < n)):
            @pl.when(ok)
            def _():
                relay(window, k).wait_send()


def attend_kernel(n, span, heads, order_ref, q_hbm, win_ref, near_ref, out_hbm, q, out, scores, bias, probs, q_sem, out_sem):
    me = lax.axis_index("ctx")
    width = (WINDOW + 1) * span
    groups = heads // HEAD_BLOCK
    blocks = 2 * groups
    chunks = width // 128
    factor = LOG2E * (KEY_DIM + ROPE_DIM) ** -0.5
    columns = HEAD_BLOCK * LATENT

    def multiple(value, of):
        return value if isinstance(value, int) else pl.multiple_of(value, of)

    def q_copy(b):
        slot, group = b // groups, b % groups
        positions = pl.ds(multiple(slot * span, 16), span)
        block_heads = pl.ds(multiple(group * HEAD_BLOCK, HEAD_BLOCK), HEAD_BLOCK)
        return pltpu.make_async_copy(q_hbm.at[positions, block_heads], q.at[b], q_sem.at[b])

    def out_copy(b):
        slot, group = b // groups, b % groups
        positions = pl.ds(multiple(slot * span, 16), span)
        return pltpu.make_async_copy(
            out.at[b], out_hbm.at[positions, pl.ds(multiple(group * columns, columns), columns)], out_sem.at[b]
        )

    for b in range(blocks):
        q_copy(b).start()
    for slot in range(2):
        span_id = order_ref[2 * me + slot]
        keypos = lax.broadcasted_iota(jnp.int32, (span, width), 1)
        row = lax.broadcasted_iota(jnp.int32, (span, width), 0)
        allowed = (keypos >= (WINDOW - span_id) * span) & (keypos - WINDOW * span <= row)
        bias[slot] = jnp.where(allowed, 0.0, -1e30)

    def window_of(b):
        return jnp.where(order_ref[2 * me + b // groups] < n, 0, 1)

    pos_part, head_part = span // PARTS, HEAD_BLOCK // PARTS

    def score(b, parity, part):
        block = q[b, part * pos_part : (part + 1) * pos_part].reshape(pos_part * HEAD_BLOCK, q.shape[3])
        product = lax.dot_general(
            block, win_ref[window_of(b), : width - 128], (((1,), (1,)), ((), ())), preferred_element_type=jnp.float32
        )
        for c in range(chunks - 1):
            for p in range(pos_part):
                first = (part * pos_part + p) * PITCH
                scores[parity * (chunks - 1) + c, first : first + HEAD_BLOCK] = product[
                    p * HEAD_BLOCK : (p + 1) * HEAD_BLOCK, c * 128 : (c + 1) * 128
                ]

    def mix(b, parity, part):
        for h in range(part * head_part, (part + 1) * head_part):
            planes = [scores.at[parity * (chunks - 1) + c] for c in range(chunks - 1)] + [near_ref.at[b]]
            tiles = [
                plane[pl.ds(h, span, stride=PITCH), :] + bias[b // groups, :, c * 128 : (c + 1) * 128]
                for c, plane in enumerate(planes)
            ]
            largest = jnp.max(functools.reduce(jnp.maximum, tiles), axis=-1, keepdims=True)
            weights = [jnp.exp2((tile - largest) * factor) for tile in tiles]
            inverse = 1.0 / jnp.sum(sum(weights), axis=-1, keepdims=True)
            for c in range(chunks):
                probs[parity, h * span : (h + 1) * span, c * 128 : (c + 1) * 128] = (weights[c] * inverse).astype(
                    jnp.bfloat16
                )
        rows = head_part * span
        mixed = jnp.dot(
            probs[parity, part * rows : (part + 1) * rows],
            win_ref[window_of(b), :, :LATENT],
            preferred_element_type=jnp.float32,
        )
        for k in range(head_part):
            h = part * head_part + k
            out[b, :, h * LATENT : (h + 1) * LATENT] = mixed[k * span : (k + 1) * span].astype(jnp.bfloat16)

    def step(b, parity, more=True):
        if more:
            q_copy(b + 1).wait()
        for part in range(PARTS):
            if more:
                score(b + 1, 1 - parity, part)
            mix(b, parity, part)
        out_copy(b).start()

    q_copy(0).wait()
    for part in range(PARTS):
        score(0, 0, part)

    @pl.loop(0, groups - 1)
    def _(pair):
        step(2 * pair, 0)
        step(2 * pair + 1, 1)

    step(blocks - 2, 0)
    step(blocks - 1, 1, more=False)
    for b in range(blocks):
        out_copy(b).wait()


def local(queries, kv_latent, span_order):
    n = lax.axis_size("ctx")
    tokens, heads, dim = queries.shape
    span = tokens // 2
    width = (WINDOW + 1) * span
    blocks = 2 * (heads // HEAD_BLOCK)
    windows, near = pl.pallas_call(
        functools.partial(gather_kernel, n, span),
        out_shape=(
            jax.ShapeDtypeStruct((2, width, dim), jnp.bfloat16),
            jax.ShapeDtypeStruct((blocks, span * PITCH, 128), jnp.float32),
        ),
        in_specs=[
            pl.BlockSpec(memory_space=pltpu.SMEM),
            pl.BlockSpec(memory_space=pltpu.VMEM),
            pl.BlockSpec(memory_space=pltpu.HBM),
        ],
        out_specs=(pl.BlockSpec(memory_space=pltpu.VMEM), pl.BlockSpec(memory_space=pltpu.VMEM)),
        scratch_shapes=[
            pltpu.VMEM((2, span, dim), jnp.bfloat16),
            pltpu.VMEM((2, 128, dim), jnp.bfloat16),
            pltpu.VMEM((blocks, span, HEAD_BLOCK, dim), jnp.bfloat16),
            pltpu.SemaphoreType.DMA((WINDOW + 1,)),
            pltpu.SemaphoreType.DMA((WINDOW + 1,)),
            pltpu.SemaphoreType.DMA((WINDOW + 1,)),
            pltpu.SemaphoreType.DMA((2, WINDOW + 1)),
            pltpu.SemaphoreType.DMA((2, WINDOW + 1)),
            pltpu.SemaphoreType.DMA((blocks,)),
        ],
        compiler_params=pltpu.CompilerParams(
            collective_id=0, has_side_effects=True, vmem_limit_bytes=48 * 1024 * 1024
        ),
        name="gather_windows",
    )(span_order, kv_latent, queries)
    return pl.pallas_call(
        functools.partial(attend_kernel, n, span, heads),
        out_shape=jax.ShapeDtypeStruct((tokens, heads * LATENT), jnp.bfloat16),
        in_specs=[
            pl.BlockSpec(memory_space=pltpu.SMEM),
            pl.BlockSpec(memory_space=pltpu.HBM),
            pl.BlockSpec(memory_space=pltpu.VMEM),
            pl.BlockSpec(memory_space=pltpu.VMEM),
        ],
        out_specs=pl.BlockSpec(memory_space=pltpu.HBM),
        scratch_shapes=[
            pltpu.VMEM((blocks, span, HEAD_BLOCK, dim), jnp.bfloat16),
            pltpu.VMEM((blocks, span, HEAD_BLOCK * LATENT), jnp.bfloat16),
            pltpu.VMEM((2 * (width // 128 - 1), span * PITCH, 128), jnp.float32),
            pltpu.VMEM((2, span, width), jnp.float32),
            pltpu.VMEM((2, span * HEAD_BLOCK, width), jnp.bfloat16),
            pltpu.SemaphoreType.DMA((blocks,)),
            pltpu.SemaphoreType.DMA((blocks,)),
        ],
        compiler_params=pltpu.CompilerParams(vmem_limit_bytes=48 * 1024 * 1024),
        name="attend",
    )(span_order, queries, windows, near)


def solution(mesh):
    in_specs = (P(("groups", "ctx"), None, None), P(("groups", "ctx"), None), P("groups"))
    out_specs = P(("groups", "ctx"), None)
    return jax.shard_map(local, mesh=mesh, in_specs=in_specs, out_specs=out_specs, check_vma=False)
```
